256 devices in a mesh: dom: 32 (over z, y_hi, core), orb: 8 (over y_lo, x).
Axes of the slice: x: 4, y: 4 (y_hi: 2, y_lo: 2; y = y_hi * 2 + y_lo), z: 8, core: 2. Of those that a mesh axis runs over, the one named last changes fastest.
Arguments:
- orbitals: float32 [192, 768, 8, 128], P('orb', 'dom')
- potential: float32 [768, 8, 128], P('dom'), may hold values from -3 to 1
- proj_index: int32 [64, 96], replicated, may hold values from 0 to 786431, as said below
- proj_values: float32 [64, 96], replicated, may hold values from -0.625 to 0.625
- proj_energy: float32 [64], replicated, may hold values from 5 to 20
Outputs:
- filtered: float32 [192, 768, 8, 128], P('orb', 'dom')
- hamiltonian_sub: float32 [192, 192], P('orb')
- correlation_sub: float32 [192, 192], P('orb')
The draws below stay inside these ranges and needn't reach their ends.
Inputs may be any that keep to these rules, and one draw needn't show every extreme that they name: `proj_index`: row a lists, ordered along the first dimension then the second then the third, the 96 cells of a box of 6 x 4 x 4 cells inside the grid; the box's first coordinate is at most 762 and otherwise lies within the slab of cells a // 2 * 24 to a // 2 * 24 + 23.
All inputs are finite; a program needn't handle non-finite values.
Results may differ from the reference program's by a relative error of at most 0.00005.
Values sent between devices are 32-bit elements; how exact they have to be, the bound alone decides.
A program may use at most 128 MiB of HBM per device.

```python
import jax
import jax.numpy as jnp
from jax import lax

ORBS = 192
CX = 24
NY = 8
NZ = 128
NX = 768
HALO = 6
ATOM_DEV = 2
ATOMS = 64
BOX_X = 6
BOX_Y = 4
BOX_Z = 4
PTS = 96
N_ORB = 8


def draw_orbitals(key, part):
    key = jax.random.fold_in(key, 3)
    key_private, key_common, key_mixing = jax.random.split(key, 3)
    full_shape = (ORBS, NX, NY, NZ)
    private = jax.random.normal(key_private, full_shape, jnp.float32)
    common = jax.random.normal(key_common, (4, NX, NY, NZ), jnp.float32)
    mixing = jax.random.uniform(key_mixing, (ORBS, 4), jnp.float32, -0.8, 0.8)
    result = private
    for index_k in range(4):
        result = result + mixing[:, index_k, None, None, None] * common[index_k][None]
    return result


def draw_proj_index(key, part):
    key = jax.random.fold_in(key, 7)
    key_x, key_y, key_z = jax.random.split(key, 3)
    atom_ids = jnp.arange(ATOMS, dtype=jnp.int32)
    owner = atom_ids // ATOM_DEV
    start_x = jnp.minimum(owner * CX + jax.random.randint(key_x, (ATOMS,), 0, CX), NX - BOX_X)
    start_y = jax.random.randint(key_y, (ATOMS,), 0, NY - BOX_Y + 1)
    start_z = jax.random.randint(key_z, (ATOMS,), 0, NZ - BOX_Z + 1)
    is_first = atom_ids == 0
    is_last = atom_ids == ATOMS - 1
    start_x = jnp.where(is_first, 0, jnp.where(is_last, NX - BOX_X, start_x))
    start_y = jnp.where(is_first, 0, jnp.where(is_last, NY - BOX_Y, start_y))
    start_z = jnp.where(is_first, 0, jnp.where(is_last, NZ - BOX_Z, start_z))
    point_ids = jnp.arange(PTS, dtype=jnp.int32)
    delta_x = point_ids // (BOX_Y * BOX_Z)
    delta_y = point_ids // BOX_Z % BOX_Y
    delta_z = point_ids % BOX_Z
    cell_x = start_x[:, None] + delta_x[None]
    cell_y = start_y[:, None] + delta_y[None]
    cell_z = start_z[:, None] + delta_z[None]
    return ((cell_x * NY + cell_y) * NZ + cell_z).astype(jnp.int32)


def steps_of(own_key, shape, pieces, low, largest):
    loudness = 1.0
    for position, shards_of in pieces:
        draws = jax.random.uniform(jax.random.fold_in(jax.random.fold_in(own_key, 6), position), (shards_of,), jnp.float32, low / len(pieces), largest / len(pieces))
        loudness = loudness * jnp.repeat(jnp.exp(draws), shape[position] // shards_of).reshape((-1,) + (1,) * (len(shape) - 1 - position))
    return loudness


def noise(rng, dims, width, limit, held_as=jnp.bfloat16):
    values = width * jax.random.normal(rng, dims, jnp.float32)
    return jnp.clip(values, min=-limit, max=limit).astype(held_as)


def setup_inputs(seed: int = 0) -> dict:
    arg_keys = jax.random.split(jax.random.key(seed), 6)
    return {
        "orbitals": draw_orbitals(jax.random.fold_in(arg_keys[5], 71), 0),
        "potential": jnp.clip(-3.0 + 4.0 * jax.random.uniform(arg_keys[1], (NX, NY, NZ), jnp.float32) ** steps_of(arg_keys[1], (NX, NY, NZ), ((0, 32),), -0.2, 0.2), -3.0, 1.0),
        "proj_index": draw_proj_index(jax.random.fold_in(arg_keys[5], 71), 0),
        "proj_values": noise(arg_keys[3], (ATOMS, PTS), PTS ** -0.5, 0.625, jnp.float32),
        "proj_energy": jnp.clip(jax.random.uniform(arg_keys[4], (ATOMS,), jnp.float32, 5.0, 20.0), 5.0, 20.0),
    }


CENTER_WEIGHT = -5369.0 / 1800.0
SIDE_WEIGHTS = (12.0 / 7.0, -15.0 / 56.0, 10.0 / 189.0, -1.0 / 112.0, 2.0 / 1925.0, -1.0 / 16632.0)
LOWER_BOUND = -1.0
CUT_BOUND = 2.0
UPPER_BOUND = 16.0
HALF_WIDTH = (UPPER_BOUND - CUT_BOUND) / 2.0
MIDDLE = (UPPER_BOUND + CUT_BOUND) / 2.0
SIGMA_ONE = HALF_WIDTH / (LOWER_BOUND - MIDDLE)
SIGMA_TWO = 1.0 / (2.0 / SIGMA_ONE - SIGMA_ONE)


def laplace(center, padded):
    slab_x, span_y, span_z = center.shape[1], center.shape[2], center.shape[3]
    wide_y = jnp.pad(center, ((0, 0), (0, 0), (HALO, HALO), (0, 0)))
    wide_z = jnp.pad(center, ((0, 0), (0, 0), (0, 0), (HALO, HALO)))
    summed = (3.0 * CENTER_WEIGHT) * center
    for shift_by in range(1, HALO + 1):
        weight = SIDE_WEIGHTS[shift_by - 1]
        neighbours = padded[:, HALO + shift_by:HALO + shift_by + slab_x] + padded[:, HALO - shift_by:HALO - shift_by + slab_x]
        neighbours = neighbours + wide_y[:, :, HALO + shift_by:HALO + shift_by + span_y] + wide_y[:, :, HALO - shift_by:HALO - shift_by + span_y]
        neighbours = neighbours + wide_z[:, :, :, HALO + shift_by:HALO + shift_by + span_z] + wide_z[:, :, :, HALO - shift_by:HALO - shift_by + span_z]
        summed = summed + weight * neighbours
    return summed


def nonlocal_terms(flat_field, proj_index, proj_values, offset):
    cell_count = flat_field.shape[1]
    local_index = proj_index - offset
    inside = (local_index >= 0) & (local_index < cell_count)
    safe_index = jnp.where(inside, local_index, 0).astype(jnp.int32)
    weights = jnp.where(inside, proj_values, jnp.zeros_like(proj_values))
    picked = flat_field[:, safe_index]
    return jnp.sum(picked * weights[None], axis=2), safe_index, weights


def add_back(flat_field, safe_index, weights, proj_energy, totals):
    spread_back = weights[None] * (proj_energy[None, :, None] * totals[:, :, None])
    return jnp.zeros_like(flat_field).at[:, safe_index].add(spread_back)


def apply_hamiltonian(field, potential, proj_index, proj_values, proj_energy):
    padded = jnp.pad(field, ((0, 0), (HALO, HALO), (0, 0), (0, 0)))
    laplacian = laplace(field, padded)
    flat_field = field.reshape(field.shape[0], -1)
    totals, safe_index, weights = nonlocal_terms(flat_field, proj_index, proj_values, 0)
    nonlocal_part = add_back(flat_field, safe_index, weights, proj_energy, totals).reshape(field.shape)
    return -0.5 * laplacian + potential[None] * field + nonlocal_part


def chebyshev(orbital_block, potential, proj_index, proj_values, proj_energy):
    image_one = apply_hamiltonian(orbital_block, potential, proj_index, proj_values, proj_energy)
    filtered_one = (SIGMA_ONE / HALF_WIDTH) * (image_one - MIDDLE * orbital_block)
    image_two = apply_hamiltonian(filtered_one, potential, proj_index, proj_values, proj_energy)
    second = (2.0 * SIGMA_TWO / HALF_WIDTH) * (image_two - MIDDLE * filtered_one) - (SIGMA_ONE * SIGMA_TWO) * orbital_block
    image_three = apply_hamiltonian(second, potential, proj_index, proj_values, proj_energy)
    return second, image_three


def reference(orbitals, potential, proj_index, proj_values, proj_energy):
    blocks = orbitals.reshape(N_ORB, ORBS // N_ORB, NX, NY, NZ)
    filtered, images = lax.map(lambda orbital_block: chebyshev(orbital_block, potential, proj_index, proj_values, proj_energy), blocks)
    filtered = filtered.reshape(ORBS, NX, NY, NZ)
    flat_filtered = filtered.reshape(ORBS, -1)
    flat_images = images.reshape(ORBS, -1)
    total_cells = NX * NY * NZ
    hamiltonian_sub = jnp.dot(flat_filtered, flat_images.T, precision=lax.Precision.HIGHEST) / total_cells
    correlation_sub = jnp.dot(flat_filtered, flat_filtered.T, precision=lax.Precision.HIGHEST) / total_cells
    return filtered, hamiltonian_sub, correlation_sub
```

```python
import functools

import jax
import jax.numpy as jnp
import numpy as np
from jax import lax
from jax.experimental import pallas as pl
from jax.experimental.pallas import tpu as pltpu
from jax.sharding import PartitionSpec as P

MESH = pl.DeviceIdType.MESH
F32 = jnp.float32
BF16 = jnp.bfloat16

CENTER_WEIGHT = -5369.0 / 1800.0
SIDE_WEIGHTS = (12.0 / 7.0, -15.0 / 56.0, 10.0 / 189.0, -1.0 / 112.0, 2.0 / 1925.0, -1.0 / 16632.0)
LOWER_BOUND = -1.0
CUT_BOUND = 2.0
UPPER_BOUND = 16.0
HALF_WIDTH = (UPPER_BOUND - CUT_BOUND) / 2.0
MIDDLE = (UPPER_BOUND + CUT_BOUND) / 2.0
SIGMA_ONE = HALF_WIDTH / (LOWER_BOUND - MIDDLE)
SIGMA_TWO = 1.0 / (2.0 / SIGMA_ONE - SIGMA_ONE)

ORB = 24
CX = 24
HALO = 6
NY = 8
NZ = 128
ROWS = CX * NY
EDGE = HALO * NY
PAD = ROWS + 2 * EDGE
NQ = 4
OQ = ORB // NQ
NX4 = 4
XL = CX // NX4
XR = XL * NY
XA, XB = 32, 16
W = NX4 * ORB
K = XR * NZ
NDOM = 32
SIDE = tuple(-0.5 * w for w in SIDE_WEIGHTS)
DIAG = -0.5 * 3.0 * CENTER_WEIGHT


def band(n):
    m = np.zeros((n, n), np.float64)
    for k, w in enumerate(SIDE, 1):
        m += w * (np.eye(n, k=k) + np.eye(n, k=-k))
    return m


def constants():
    bz = jnp.asarray(band(NZ), F32)
    hi = bz.astype(BF16)
    lo = (bz - hi.astype(F32)).astype(BF16)
    wz = jnp.concatenate(
        [jnp.concatenate([hi, lo], 1), jnp.concatenate([hi, jnp.zeros_like(lo)], 1)], 0
    )
    by = band(NY)
    cy = np.zeros((NY, NY, NZ), np.float32)
    for s in range(NY):
        for y in range(NY):
            cy[s, y, :] = by[y, (y - s) % NY]
    return wz, jnp.asarray(cy)


def kernel(
    x_ref, pot_ref, idx_ref, val_ref, en_ref, wz_ref, cy_ref,
    out_ref, gram_ref,
    p0, p1, p2, im, cf, box, dfo, dfp, tb, pe,
    fa, ia, fo, fb, ib, ob, snd_own, snd_x, rcv_own, rcv_x, red, a2, a3, mine,
    loc_sem, hs, hr, fs, fr, gs, gr, ys, yr, vs, vr, r1s, r1r, r2s, r2r, r3s, r3r, r4s, r4r,
):
    dom = lax.axis_index("dom")
    orb = lax.axis_index("orb")
    row = orb // NX4
    xx = orb % NX4
    zz = dom // 4
    tt = dom % 4
    up = lax.rem(dom + 1, NDOM)
    down = lax.rem(dom + NDOM - 1, NDOM)
    other = (1 - row) * NX4

    def xpeer(k):
        return lax.rem(xx + k, NX4)

    barrier = pltpu.get_barrier_semaphore()
    peers = [(up, orb), (down, orb)]
    peers += [(dom, row * NX4 + xpeer(k)) for k in range(1, 4)]
    peers += [(dom, other + xpeer(k)) for k in range(4)]
    peers += [(zz * 4 + lax.rem(tt + k, 4), orb) for k in range(1, 4)]
    peers += [(lax.rem(zz + k, 8) * 4 + tt, orb) for k in range(1, 8)]
    for peer in peers:
        pl.semaphore_signal(barrier, inc=1, device_id=peer, device_id_type=MESH)

    load = pltpu.make_async_copy(x_ref, p0.at[:, pl.ds(EDGE, ROWS), :], loc_sem.at[0])
    load.start()
    pl.semaphore_wait(barrier, len(peers))

    def remote(src, dst, send, recv, device):
        return pltpu.make_async_remote_copy(
            src_ref=src, dst_ref=dst, send_sem=send, recv_sem=recv, device_id=device, device_id_type=MESH
        )

    def halo(field, src, base, q, way):
        part = pl.ds(q * OQ, OQ)
        if way == 0:
            s = src.at[part, pl.ds(base + ROWS - EDGE, EDGE), :]
            d = (p0, p1, p2)[field].at[part, pl.ds(0, EDGE), :]
            to = (up, orb)
        else:
            s = src.at[part, pl.ds(base, EDGE), :]
            d = (p0, p1, p2)[field].at[part, pl.ds(EDGE + ROWS, EDGE), :]
            to = (down, orb)
        return remote(s, d, hs.at[field, way, q], hr.at[field, way, q], to)

    def halo_start(field, src, base, q):
        @pl.when(dom < NDOM - 1)
        def _():
            halo(field, src, base, q, 0).start()

        @pl.when(dom > 0)
        def _():
            halo(field, src, base, q, 1).start()

    def halo_recv(field, src, base, q):
        @pl.when(dom > 0)
        def _():
            halo(field, src, base, q, 0).wait_recv()

        @pl.when(dom < NDOM - 1)
        def _():
            halo(field, src, base, q, 1).wait_recv()

    def halo_sent(field, src, base, q):
        @pl.when(dom < NDOM - 1)
        def _():
            halo(field, src, base, q, 0).wait_send()

        @pl.when(dom > 0)
        def _():
            halo(field, src, base, q, 1).wait_send()

    def loop(n, body):
        lax.fori_loop(0, n, lambda i, c: (body(i), c)[1], 0)

    loop(NQ, lambda q: halo_start(0, x_ref, 0, q))

    @pl.when(dom == 0)
    def _():
        for p in (p0, p1, p2):
            p[:, 0:EDGE, :] = jnp.zeros((ORB, EDGE, NZ), F32)

    @pl.when(dom == NDOM - 1)
    def _():
        for p in (p0, p1, p2):
            p[:, EDGE + ROWS :, :] = jnp.zeros((ORB, EDGE, NZ), F32)

    cf[...] = pot_ref[...] + (DIAG - MIDDLE)
    for buf in (fb, ib, ob):
        for h in (0, 128):
            buf[h + W : h + 128, :] = jnp.zeros((128 - W, buf.shape[1]), BF16)

    sub = lax.broadcasted_iota(jnp.int32, (NY, NZ), 0)
    lane = lax.broadcasted_iota(jnp.int32, (NY, NZ), 1)

    def atom_id(a):
        return jnp.where(a < 2, 2 * dom + a, jnp.maximum(2 * dom - 4 + a, 0))

    def start_of(a):
        first = idx_ref[atom_id(a), 0]
        return first // (NY * NZ) - CX * dom, first // NZ % NY, first % NZ

    def build_box(a):
        _, y0, z0 = start_of(a)
        dy = sub - y0
        dz = lane - z0

        def layer(l):
            d = jnp.zeros((NY, NZ), F32)
            for j in range(4):
                for k in range(4):
                    d = jnp.where((dy == j) & (dz == k), val_ref[atom_id(a), l * 16 + j * 4 + k], d)
            box[a, l] = d

        loop(6, layer)

    loop(4, build_box)

    def place(a, x):
        x0, _, _ = start_of(a)
        off = jnp.zeros((NY, NZ), jnp.int32) + (x - x0)
        d = jnp.zeros((NY, NZ), F32)
        for l in range(6):
            d = jnp.where(off == l, box[a, l], d)
        return d

    def place_own(x):
        for a in range(2):
            dfo[a, x] = place(a, x)

    def place_low(i):
        for a in range(2):
            dfp[a, i] = place(a + 2, i - 5)

    loop(29, place_own)
    loop(10, place_low)

    def inner(p, n):
        def body(o):
            c = p[o, EDGE : EDGE + ROWS, :]
            hi = c.astype(BF16)
            lo = (c - hi.astype(F32)).astype(BF16)
            z = jnp.dot(jnp.concatenate([hi, lo], 1), wz_ref[...], preferred_element_type=F32)
            z = z[:, :NZ] + z[:, NZ:]
            t = [jnp.zeros((NY, NZ), F32)] * 4
            for x0 in range(0, CX, 8):
                first, last = max(x0 - HALO, 0), min(x0 + 8 + HALO, CX)
                blk = p[o, EDGE + first * NY : EDGE + last * NY, :].reshape(last - first, NY, NZ)
                zero = jnp.zeros((8 + 2 * HALO - (last - first), NY, NZ), F32)
                if x0 - HALO < 0:
                    blk = jnp.concatenate([zero, blk], 0)
                elif x0 + 8 + HALO > CX:
                    blk = jnp.concatenate([blk, zero], 0)
                ctr = blk[HALO : HALO + 8]
                rows = slice(x0 * NY, (x0 + 8) * NY)
                s = cf[rows, :].reshape(8, NY, NZ) * ctr + z[rows, :].reshape(8, NY, NZ)
                for k in range(1, HALO + 1):
                    s = s + SIDE[k - 1] * (blk[HALO + k : HALO + 8 + k] + blk[HALO - k : HALO + 8 - k])
                for r in range(1, NY):
                    s = s + cy_ref[r][None] * pltpu.roll(ctr, r, 1)
                n[o, pl.ds(EDGE + x0 * NY, 8 * NY), :] = s.reshape(8 * NY, NZ)
                for a in range(2):
                    t[a] = t[a] + jnp.sum(dfo[a, x0 : x0 + 8] * ctr, axis=0)
                    if x0 == 0:
                        t[2 + a] = jnp.sum(dfp[a, 5:10] * ctr[0:5], axis=0)
            for a in range(4):
                tb[o, a] = t[a]

        loop(ORB, body)

    def outer(p, n, q, scale, extra):
        def body(i):
            o = q * OQ + i
            low = p[o, 0:EDGE, :].reshape(HALO, NY, NZ)
            high = p[o, EDGE + ROWS : PAD, :].reshape(HALO, NY, NZ)
            for a in range(2):
                tb[o, a] = tb[o, a] + jnp.sum(dfo[a, 24:29] * high[0:5], axis=0)
                tb[o, 2 + a] = tb[o, 2 + a] + jnp.sum(dfp[a, 0:5] * low[1:6], axis=0)
            first = [jnp.zeros((NY, NZ), F32)] * HALO
            last = [jnp.zeros((NY, NZ), F32)] * HALO
            for k in range(1, HALO + 1):
                for x in range(k):
                    first[x] = first[x] + SIDE[k - 1] * low[HALO - k + x]
                    last[HALO - k + x] = last[HALO - k + x] + SIDE[k - 1] * high[x]
            add = jnp.concatenate(first, 0)
            n[o, pl.ds(EDGE, EDGE), :] = n[o, pl.ds(EDGE, EDGE), :] + add
            add = jnp.concatenate(last, 0)
            n[o, pl.ds(ROWS, EDGE), :] = n[o, pl.ds(ROWS, EDGE), :] + add

        loop(OQ, body)
        part = pl.ds(q * OQ, OQ)
        total = jnp.sum(jnp.sum(tb[part], axis=3, keepdims=True), axis=2, keepdims=True)
        for a in range(4):
            e = en_ref[0, atom_id(a)]
            if a >= 2:
                e = jnp.where(dom > 0, e, 0.0)
            pe[part, a] = jnp.broadcast_to(total[:, a] * e, (OQ, NY, NZ))

        def finish(i):
            o = q * OQ + i
            for x0 in range(0, CX, 8):
                rows = pl.ds(EDGE + x0 * NY, 8 * NY)
                s = n[o, rows, :].reshape(8, NY, NZ)
                for a in range(2):
                    s = s + dfo[a, x0 : x0 + 8] * pe[o, a][None]
                if x0 == 0:
                    t = s[0:5]
                    for a in range(2):
                        t = t + dfp[a, 5:10] * pe[o, 2 + a][None]
                    s = jnp.concatenate([t, s[5:8]], 0)
                if extra == 2:
                    s = scale * s - (SIGMA_ONE * SIGMA_TWO) * p0[o, rows, :].reshape(8, NY, NZ)
                elif extra == 1:
                    s = scale * s
                else:
                    s = s + MIDDLE * p[o, rows, :].reshape(8, NY, NZ)
                n[o, rows, :] = s.reshape(8 * NY, NZ)

        loop(OQ, finish)

    load.wait()
    inner(p0, p1)

    def step_one(q):
        halo_recv(0, x_ref, 0, q)
        outer(p0, p1, q, SIGMA_ONE / HALF_WIDTH, 1)
        halo_start(1, p1, EDGE, q)

    loop(NQ, step_one)

    def gather(src, dst, send, recv, q, k):
        s = src.at[pl.ds(q * OQ, OQ), pl.ds(pl.multiple_of(EDGE + xpeer(k) * XR, 8), XR), :]
        d = dst.at[pl.ds(xx * ORB + q * OQ, OQ), :, :]
        return remote(s, d, send.at[q, k], recv.at[q, k], (dom, row * NX4 + xpeer(k)))

    def keep(src, dst, sem, q):
        s = src.at[pl.ds(q * OQ, OQ), pl.ds(pl.multiple_of(EDGE + xx * XR, 8), XR), :]
        return pltpu.make_async_copy(s, dst.at[pl.ds(xx * ORB + q * OQ, OQ), :, :], sem)

    def store(q):
        part = pl.ds(q * OQ, OQ)
        return pltpu.make_async_copy(
            p2.at[part, pl.ds(EDGE, ROWS), :], out_ref.at[part, :, :], loc_sem.at[1 + q]
        )

    def cross(src, to, rows, q, k, send, recv):
        who = lax.rem(xx + NX4 - k, NX4)
        part = pl.ds(who * ORB + q * OQ, OQ)
        return remote(
            src.at[part, rows, :], fo.at[part, to, :], send.at[q, k], recv.at[q, k], (dom, other + xx)
        )

    def cross_low(q, k):
        return cross(fa, pl.ds(0, XA), pl.ds(0, XA), q, k, ys, yr)

    def cross_high(q, k):
        return cross(fa, pl.ds(0, XB), pl.ds(XA, XB), q, k, ys, yr)

    def cross_image(q, k):
        return cross(ia, pl.ds(XB, XB), pl.ds(XA, XB), q, k, vs, vr)

    def by_row(zero, one):
        if zero is not None:
            pl.when(row == 0)(zero)
        if one is not None:
            pl.when(row == 1)(one)

    inner(p1, p2)

    def step_two(q):
        halo_recv(1, p1, EDGE, q)
        outer(p1, p2, q, 2.0 * SIGMA_TWO / HALF_WIDTH, 2)
        halo_start(2, p2, EDGE, q)
        for k in range(1, 4):
            gather(p2, fa, fs, fr, q, k).start()
        keep(p2, fa, fs.at[q, 0], q).start()
        store(q).start()

    loop(NQ, step_two)

    inner(p2, im)

    def step_three(q):
        halo_recv(2, p2, EDGE, q)
        outer(p2, im, q, 1.0, 0)
        for k in range(1, 4):
            gather(im, ia, gs, gr, q, k).start()
        keep(im, ia, gs.at[q, 0], q).start()

    loop(NQ, step_three)

    def pass_on(q):
        keep(p2, fa, fs.at[q, 0], q).wait()
        for k in range(4):
            if k:
                gather(p2, fa, fs, fr, q, k).wait_recv()
            by_row(lambda: cross_high(q, k).start(), lambda: cross_low(q, k).start())

    loop(NQ, pass_on)

    def arrived(q):
        for k in range(4):
            by_row(lambda: cross_low(q, k).wait_recv(), lambda: cross_high(q, k).wait_recv())

    def split(src, height, dst, start, rows):
        flat = src.reshape(W * height, NZ)

        def body(c):
            v = [flat[pl.ds(start + 2 * c + i, W, stride=height), :] for i in range(2)]
            v = jnp.concatenate(v, 1)
            hi = v.astype(BF16)
            at = pl.ds(pl.multiple_of(c * 2 * NZ, 2 * NZ), 2 * NZ)
            dst[0:W, at] = hi
            dst[128 : 128 + W, at] = (v - hi.astype(F32)).astype(BF16)

        loop(rows // 2, body)

    def mul(a, b):
        g = lax.dot_general(a, b, (((1,), (1,)), ((), ())), preferred_element_type=F32)
        g = g[:128] + g[128:]
        return g[:, :128] + g[:, 128:]

    def put(m, h, g):
        snd_own[:, 2 * m + h] = g[:W].reshape(NX4, ORB, 128)
        if h:
            snd_x[:, m] = jnp.transpose(g)[:W].reshape(NX4, ORB, 128)

    split(fa, XR, fb, 0, XR)
    put(1, 0, mul(fb[...], fb[...]))
    loop(NQ, arrived)

    def across_zero():
        split(fo, XA, ob, 0, XA)
        put(1, 1, mul(fb[:, : XA * NZ], ob[...]))

    def across_one():
        split(fo, XA, ob, 0, XB)
        put(1, 1, mul(fb[:, XA * NZ :], ob[:, : XB * NZ]))

    by_row(across_zero, across_one)

    def image_in(q):
        keep(im, ia, gs.at[q, 0], q).wait()
        for k in range(4):
            if k:
                gather(im, ia, gs, gr, q, k).wait_recv()
            by_row(lambda: cross_image(q, k).start(), None)

    loop(NQ, image_in)
    split(ia, XR, ib, 0, XR)
    put(0, 0, mul(ib[...], fb[...]))

    def image_zero():
        put(0, 1, mul(ib[:, : XA * NZ], ob[...]))

    def image_one():
        def wait(q):
            for k in range(4):
                cross_image(q, k).wait_recv()

        loop(NQ, wait)
        split(fo, XA, ob, XB, XB)
        put(0, 1, mul(fb[:, XA * NZ :], ob[:, : XB * NZ]))

    by_row(image_zero, image_one)

    def rows_own(k):
        return remote(
            snd_own.at[xpeer(k)], rcv_own.at[k], r1s.at[k], r1r.at[k], (dom, row * NX4 + xpeer(k))
        )

    def rows_x(k):
        return remote(
            snd_x.at[xpeer(k)], rcv_x.at[k], r1s.at[4 + k], r1r.at[4 + k], (dom, other + xpeer(k))
        )

    for k in range(4):
        rows_x(k).start()
    for k in range(1, 4):
        rows_own(k).start()
    total = snd_own[xx]
    for k in range(1, 4):
        rows_own(k).wait_recv()
        total = total + rcv_own[k]
    cr = jnp.zeros((2, ORB, 128), F32)
    for k in range(4):
        rows_x(k).wait_recv()
        cr = cr + rcv_x[k]
    red[...] = total
    red[1] = total[1] + cr[0]
    red[3] = total[3] + cr[1]

    def quarter(k):
        t = lax.rem(tt + k, 4)
        return remote(red.at[t], a2.at[k], r2s.at[k], r2r.at[k], (zz * 4 + t, orb))

    for k in range(1, 4):
        quarter(k).start()
    s = red[tt]
    for k in range(1, 4):
        quarter(k).wait_recv()
        s = s + a2[k]
    mine[...] = s

    def along(k):
        z = lax.rem(zz + k, 8)
        return remote(mine, a3.at[k], r3s.at[k], r3r.at[k], (z * 4 + tt, orb))

    for k in range(1, 8):
        along(k).start()
    for k in range(1, 8):
        along(k).wait_recv()
        s = s + a3[k]
    gram_ref[tt] = s

    def back(k):
        t = lax.rem(tt + k, 4)
        return remote(gram_ref.at[tt], gram_ref.at[tt], r4s.at[k], r4r.at[k], (zz * 4 + t, orb))

    for k in range(1, 4):
        back(k).start()

    def sent(q):
        halo_sent(0, x_ref, 0, q)
        halo_sent(1, p1, EDGE, q)
        halo_sent(2, p2, EDGE, q)
        store(q).wait()
        for k in range(1, 4):
            gather(p2, fa, fs, fr, q, k).wait_send()
            gather(im, ia, gs, gr, q, k).wait_send()
        for k in range(4):
            by_row(lambda: cross_high(q, k).wait_send(), lambda: cross_low(q, k).wait_send())
            by_row(lambda: cross_image(q, k).wait_send(), None)

    loop(NQ, sent)
    for k in range(1, 4):
        rows_own(k).wait_send()
        quarter(k).wait_send()
        back(k).wait_send()
    for k in range(4):
        rows_x(k).wait_send()
    for k in range(1, 8):
        along(k).wait_send()
    for k in range(1, 4):
        t = lax.rem(tt + 4 - k, 4)
        remote(
            gram_ref.at[t], gram_ref.at[t], r4s.at[k], r4r.at[k], (zz * 4 + t, orb)
        ).wait_recv()


def on_device(orbitals, potential, proj_index, proj_values, proj_energy):
    wz, cy = constants()
    dma = pltpu.SemaphoreType.DMA
    vmem = pl.BlockSpec(memory_space=pltpu.VMEM)
    smem = pl.BlockSpec(memory_space=pltpu.SMEM)
    hbm = pl.BlockSpec(memory_space=pl.ANY)
    filtered, gram = pl.pallas_call(
        kernel,
        out_shape=(
            jax.ShapeDtypeStruct((ORB, ROWS, NZ), F32),
            jax.ShapeDtypeStruct((4, ORB, 128), F32),
        ),
        in_specs=[hbm, vmem, smem, smem, smem, vmem, vmem],
        out_specs=(hbm, vmem),
        scratch_shapes=[
            pltpu.VMEM((ORB, PAD, NZ), F32),
            pltpu.VMEM((ORB, PAD, NZ), F32),
            pltpu.VMEM((ORB, PAD, NZ), F32),
            pltpu.VMEM((ORB, PAD, NZ), F32),
            pltpu.VMEM((ROWS, NZ), F32),
            pltpu.VMEM((4, 6, NY, NZ), F32),
            pltpu.VMEM((2, 29, NY, NZ), F32),
            pltpu.VMEM((2, 10, NY, NZ), F32),
            pltpu.VMEM((ORB, 4, NY, NZ), F32),
            pltpu.VMEM((ORB, 4, NY, NZ), F32),
            pltpu.VMEM((W, XR, NZ), F32),
            pltpu.VMEM((W, XR, NZ), F32),
            pltpu.VMEM((W, XA, NZ), F32),
            pltpu.VMEM((256, K), BF16),
            pltpu.VMEM((256, K), BF16),
            pltpu.VMEM((256, XA * NZ), BF16),
            pltpu.VMEM((NX4, 4, ORB, 128), F32),
            pltpu.VMEM((NX4, 2, ORB, 128), F32),
            pltpu.VMEM((NX4, 4, ORB, 128), F32),
            pltpu.VMEM((NX4, 2, ORB, 128), F32),
            pltpu.VMEM((4, ORB, 128), F32),
            pltpu.VMEM((4, ORB, 128), F32),
            pltpu.VMEM((8, ORB, 128), F32),
            pltpu.VMEM((ORB, 128), F32),
            dma((1 + NQ,)),
            dma((3, 2, NQ)), dma((3, 2, NQ)),
            dma((NQ, 4)), dma((NQ, 4)),
            dma((NQ, 4)), dma((NQ, 4)),
            dma((NQ, 4)), dma((NQ, 4)),
            dma((NQ, 4)), dma((NQ, 4)),
            dma((8,)), dma((8,)),
            dma((4,)), dma((4,)),
            dma((8,)), dma((8,)),
            dma((4,)), dma((4,)),
        ],
        compiler_params=pltpu.CompilerParams(
            collective_id=0, has_side_effects=True, vmem_limit_bytes=56 << 20
        ),
        name="filter_step",
    )(
        orbitals.reshape(ORB, ROWS, NZ),
        potential.reshape(ROWS, NZ),
        proj_index,
        proj_values,
        proj_energy.reshape(1, -1),
        wz,
        cy,
    )
    first = lax.axis_index("orb") < NX4
    cells = ROWS * NZ * lax.axis_size("dom")

    def whole(own, across):
        own, across = own[:, :W], across[:, :W]
        low = jnp.where(first, own, across)
        high = jnp.where(first, across, own)
        return jnp.concatenate([low, high], 1) / cells

    return filtered.reshape(orbitals.shape), whole(gram[0], gram[1]), whole(gram[2], gram[3])


def solution(mesh):
    in_specs = (P("orb", "dom", None, None), P("dom", None, None), P(), P(), P())
    out_specs = (P("orb", "dom", None, None), P("orb", None), P("orb", None))
    return jax.shard_map(
        on_device, mesh=mesh, in_specs=in_specs, out_specs=out_specs, check_vma=False
    )
```

```python
import functools

import jax
import jax.numpy as jnp
import numpy as np
from jax import lax
from jax.experimental import pallas as pl
from jax.experimental.pallas import tpu as pltpu
from jax.sharding import PartitionSpec as P

MESH = pl.DeviceIdType.MESH
F32 = jnp.float32
BF16 = jnp.bfloat16

CENTER_WEIGHT = -5369.0 / 1800.0
SIDE_WEIGHTS = (12.0 / 7.0, -15.0 / 56.0, 10.0 / 189.0, -1.0 / 112.0, 2.0 / 1925.0, -1.0 / 16632.0)
LOWER_BOUND = -1.0
CUT_BOUND = 2.0
UPPER_BOUND = 16.0
HALF_WIDTH = (UPPER_BOUND - CUT_BOUND) / 2.0
MIDDLE = (UPPER_BOUND + CUT_BOUND) / 2.0
SIGMA_ONE = HALF_WIDTH / (LOWER_BOUND - MIDDLE)
SIGMA_TWO = 1.0 / (2.0 / SIGMA_ONE - SIGMA_ONE)

ORB = 24
CX = 24
HALO = 6
NY = 8
NZ = 128
ROWS = CX * NY
EDGE = HALO * NY
PAD = ROWS + 2 * EDGE
NQ = 4
OQ = ORB // NQ
NX4 = 4
XL = CX // NX4
XR = XL * NY
XA, XB = 32, 16
W = NX4 * ORB
K = XR * NZ
NDOM = 32
SIDE = tuple(-0.5 * w for w in SIDE_WEIGHTS)
DIAG = -0.5 * 3.0 * CENTER_WEIGHT


def band(n):
    m = np.zeros((n, n), np.float64)
    for k, w in enumerate(SIDE, 1):
        m += w * (np.eye(n, k=k) + np.eye(n, k=-k))
    return m


def constants():
    bz = jnp.asarray(band(NZ), F32)
    hi = bz.astype(BF16)
    lo = (bz - hi.astype(F32)).astype(BF16)
    wz = jnp.concatenate(
        [jnp.concatenate([hi, lo], 1), jnp.concatenate([hi, jnp.zeros_like(lo)], 1)], 0
    )
    by = band(NY)
    cy = np.zeros((NY, NY, NZ), np.float32)
    for s in range(NY):
        for y in range(NY):
            cy[s, y, :] = by[y, (y - s) % NY]
    return wz, jnp.asarray(cy)


def kernel(
    x_ref, pot_ref, idx_ref, val_ref, en_ref, wz_ref, cy_ref,
    out_ref, gram_ref,
    p0, p1, p2, im, cf, box, dfo, dfp, tb, pe,
    fa, ia, fo, fb, ib, ob, snd_own, snd_x, rcv_own, rcv_x, red, a2, a3, mine,
    loc_sem, hs, hr, fs, fr, gs, gr, ys, yr, vs, vr, r1s, r1r, r2s, r2r, r3s, r3r, r4s, r4r,
):
    dom = lax.axis_index("dom")
    orb = lax.axis_index("orb")
    row = orb // NX4
    xx = orb % NX4
    zz = dom // 4
    tt = dom % 4
    up = lax.rem(dom + 1, NDOM)
    down = lax.rem(dom + NDOM - 1, NDOM)
    other = (1 - row) * NX4

    def xpeer(k):
        return lax.rem(xx + k, NX4)

    barrier = pltpu.get_barrier_semaphore()
    peers = [(up, orb), (down, orb)]
    peers += [(dom, row * NX4 + xpeer(k)) for k in range(1, 4)]
    peers += [(dom, other + xpeer(k)) for k in range(4)]
    peers += [(zz * 4 + lax.rem(tt + k, 4), orb) for k in range(1, 4)]
    peers += [(lax.rem(zz + k, 8) * 4 + tt, orb) for k in range(1, 8)]
    for peer in peers:
        pl.semaphore_signal(barrier, inc=1, device_id=peer, device_id_type=MESH)

    load = pltpu.make_async_copy(x_ref, p0.at[:, pl.ds(EDGE, ROWS), :], loc_sem.at[0])
    load.start()
    pl.semaphore_wait(barrier, len(peers))

    def remote(src, dst, send, recv, device):
        return pltpu.make_async_remote_copy(
            src_ref=src, dst_ref=dst, send_sem=send, recv_sem=recv, device_id=device, device_id_type=MESH
        )

    def halo(field, src, base, q, way):
        part = pl.ds(q * OQ, OQ)
        if way == 0:
            s = src.at[part, pl.ds(base + ROWS - EDGE, EDGE), :]
            d = (p0, p1, p2)[field].at[part, pl.ds(0, EDGE), :]
            to = (up, orb)
        else:
            s = src.at[part, pl.ds(base, EDGE), :]
            d = (p0, p1, p2)[field].at[part, pl.ds(EDGE + ROWS, EDGE), :]
            to = (down, orb)
        return remote(s, d, hs.at[field, way, q], hr.at[field, way, q], to)

    def halo_start(field, src, base, q):
        @pl.when(dom < NDOM - 1)
        def _():
            halo(field, src, base, q, 0).start()

        @pl.when(dom > 0)
        def _():
            halo(field, src, base, q, 1).start()

    def halo_recv(field, src, base, q):
        @pl.when(dom > 0)
        def _():
            halo(field, src, base, q, 0).wait_recv()

        @pl.when(dom < NDOM - 1)
        def _():
            halo(field, src, base, q, 1).wait_recv()

    def halo_sent(field, src, base, q):
        @pl.when(dom < NDOM - 1)
        def _():
            halo(field, src, base, q, 0).wait_send()

        @pl.when(dom > 0)
        def _():
            halo(field, src, base, q, 1).wait_send()

    def loop(n, body):
        lax.fori_loop(0, n, lambda i, c: (body(i), c)[1], 0)

    loop(2, lambda q: halo_start(0, x_ref, 0, q))

    @pl.when(dom == 0)
    def _():
        for p in (p0, p1, p2):
            p[:, 0:EDGE, :] = jnp.zeros((ORB, EDGE, NZ), F32)

    @pl.when(dom == NDOM - 1)
    def _():
        for p in (p0, p1, p2):
            p[:, EDGE + ROWS :, :] = jnp.zeros((ORB, EDGE, NZ), F32)

    cf[...] = pot_ref[...] + (DIAG - MIDDLE)
    for buf in (fb, ib, ob):
        for h in (0, 128):
            buf[h + W : h + 128, :] = jnp.zeros((128 - W, buf.shape[1]), BF16)

    sub = lax.broadcasted_iota(jnp.int32, (NY, NZ), 0)
    lane = lax.broadcasted_iota(jnp.int32, (NY, NZ), 1)

    def atom_id(a):
        return jnp.where(a < 2, 2 * dom + a, jnp.maximum(2 * dom - 4 + a, 0))

    def start_of(a):
        first = idx_ref[atom_id(a), 0]
        return first // (NY * NZ) - CX * dom, first // NZ % NY, first % NZ

    def build_box(a):
        _, y0, z0 = start_of(a)
        dy = sub - y0
        dz = lane - z0

        def layer(l):
            d = jnp.zeros((NY, NZ), F32)
            for j in range(4):
                for k in range(4):
                    d = jnp.where((dy == j) & (dz == k), val_ref[atom_id(a), l * 16 + j * 4 + k], d)
            box[a, l] = d

        loop(6, layer)

    loop(4, build_box)

    def place(a, x):
        x0, _, _ = start_of(a)
        off = jnp.zeros((NY, NZ), jnp.int32) + (x - x0)
        d = jnp.zeros((NY, NZ), F32)
        for l in range(6):
            d = jnp.where(off == l, box[a, l], d)
        return d

    def place_own(x):
        for a in range(2):
            dfo[a, x] = place(a, x)

    def place_low(i):
        for a in range(2):
            dfp[a, i] = place(a + 2, i - 5)

    loop(29, place_own)
    loop(10, place_low)

    def inner(p, n, q):
        def body(i):
            o = q * OQ + i
            c = p[o, EDGE : EDGE + ROWS, :]
            hi = c.astype(BF16)
            lo = (c - hi.astype(F32)).astype(BF16)
            z = jnp.dot(jnp.concatenate([hi, lo], 1), wz_ref[...], preferred_element_type=F32)
            z = z[:, :NZ] + z[:, NZ:]
            t = [jnp.zeros((NY, NZ), F32)] * 4
            for x0 in range(0, CX, 8):
                first, last = max(x0 - HALO, 0), min(x0 + 8 + HALO, CX)
                blk = p[o, EDGE + first * NY : EDGE + last * NY, :].reshape(last - first, NY, NZ)
                zero = jnp.zeros((8 + 2 * HALO - (last - first), NY, NZ), F32)
                if x0 - HALO < 0:
                    blk = jnp.concatenate([zero, blk], 0)
                elif x0 + 8 + HALO > CX:
                    blk = jnp.concatenate([blk, zero], 0)
                ctr = blk[HALO : HALO + 8]
                rows = slice(x0 * NY, (x0 + 8) * NY)
                s = cf[rows, :].reshape(8, NY, NZ) * ctr + z[rows, :].reshape(8, NY, NZ)
                for k in range(1, HALO + 1):
                    s = s + SIDE[k - 1] * (blk[HALO + k : HALO + 8 + k] + blk[HALO - k : HALO + 8 - k])
                for r in range(1, NY):
                    s = s + cy_ref[r][None] * pltpu.roll(ctr, r, 1)
                n[o, pl.ds(EDGE + x0 * NY, 8 * NY), :] = s.reshape(8 * NY, NZ)
                for a in range(2):
                    t[a] = t[a] + jnp.sum(dfo[a, x0 : x0 + 8] * ctr, axis=0)
                    if x0 == 0:
                        t[2 + a] = jnp.sum(dfp[a, 5:10] * ctr[0:5], axis=0)
            for a in range(4):
                tb[o, a] = t[a]

        loop(OQ, body)

    def outer(p, n, q, scale, extra):
        def body(i):
            o = q * OQ + i
            low = p[o, 0:EDGE, :].reshape(HALO, NY, NZ)
            high = p[o, EDGE + ROWS : PAD, :].reshape(HALO, NY, NZ)
            for a in range(2):
                tb[o, a] = tb[o, a] + jnp.sum(dfo[a, 24:29] * high[0:5], axis=0)
                tb[o, 2 + a] = tb[o, 2 + a] + jnp.sum(dfp[a, 0:5] * low[1:6], axis=0)
            first = [jnp.zeros((NY, NZ), F32)] * HALO
            last = [jnp.zeros((NY, NZ), F32)] * HALO
            for k in range(1, HALO + 1):
                for x in range(k):
                    first[x] = first[x] + SIDE[k - 1] * low[HALO - k + x]
                    last[HALO - k + x] = last[HALO - k + x] + SIDE[k - 1] * high[x]
            add = jnp.concatenate(first, 0)
            n[o, pl.ds(EDGE, EDGE), :] = n[o, pl.ds(EDGE, EDGE), :] + add
            add = jnp.concatenate(last, 0)
            n[o, pl.ds(ROWS, EDGE), :] = n[o, pl.ds(ROWS, EDGE), :] + add

        loop(OQ, body)
        part = pl.ds(q * OQ, OQ)
        total = jnp.sum(jnp.sum(tb[part], axis=3, keepdims=True), axis=2, keepdims=True)
        for a in range(4):
            e = en_ref[0, atom_id(a)]
            if a >= 2:
                e = jnp.where(dom > 0, e, 0.0)
            pe[part, a] = jnp.broadcast_to(total[:, a] * e, (OQ, NY, NZ))

        def finish(i):
            o = q * OQ + i
            for x0 in range(0, CX, 8):
                rows = pl.ds(EDGE + x0 * NY, 8 * NY)
                s = n[o, rows, :].reshape(8, NY, NZ)
                for a in range(2):
                    s = s + dfo[a, x0 : x0 + 8] * pe[o, a][None]
                if x0 == 0:
                    t = s[0:5]
                    for a in range(2):
                        t = t + dfp[a, 5:10] * pe[o, 2 + a][None]
                    s = jnp.concatenate([t, s[5:8]], 0)
                if extra == 2:
                    s = scale * s - (SIGMA_ONE * SIGMA_TWO) * p0[o, rows, :].reshape(8, NY, NZ)
                elif extra == 1:
                    s = scale * s
                else:
                    s = s + MIDDLE * p[o, rows, :].reshape(8, NY, NZ)
                n[o, rows, :] = s.reshape(8 * NY, NZ)

        loop(OQ, finish)

    def gather(src, dst, send, recv, q, k):
        s = src.at[pl.ds(q * OQ, OQ), pl.ds(pl.multiple_of(EDGE + xpeer(k) * XR, 8), XR), :]
        d = dst.at[pl.ds(xx * ORB + q * OQ, OQ), :, :]
        return remote(s, d, send.at[q, k], recv.at[q, k], (dom, row * NX4 + xpeer(k)))

    def keep(src, dst, sem, q):
        s = src.at[pl.ds(q * OQ, OQ), pl.ds(pl.multiple_of(EDGE + xx * XR, 8), XR), :]
        return pltpu.make_async_copy(s, dst.at[pl.ds(xx * ORB + q * OQ, OQ), :, :], sem)

    def store(q):
        part = pl.ds(q * OQ, OQ)
        return pltpu.make_async_copy(
            p2.at[part, pl.ds(EDGE, ROWS), :], out_ref.at[part, :, :], loc_sem.at[1 + q]
        )

    def cross(src, to, rows, q, k, send, recv):
        who = lax.rem(xx + NX4 - k, NX4)
        part = pl.ds(who * ORB + q * OQ, OQ)
        return remote(
            src.at[part, rows, :], fo.at[part, to, :], send.at[q, k], recv.at[q, k], (dom, other + xx)
        )

    def cross_low(q, k):
        return cross(fa, pl.ds(0, XA), pl.ds(0, XA), q, k, ys, yr)

    def cross_high(q, k):
        return cross(fa, pl.ds(0, XB), pl.ds(XA, XB), q, k, ys, yr)

    def cross_image(q, k):
        return cross(ia, pl.ds(XB, XB), pl.ds(XA, XB), q, k, vs, vr)

    def by_row(zero, one):
        if zero is not None:
            pl.when(row == 0)(zero)
        if one is not None:
            pl.when(row == 1)(one)

    def step_one(q):
        halo_recv(0, x_ref, 0, q)
        outer(p0, p1, q, SIGMA_ONE / HALF_WIDTH, 1)
        halo_start(1, p1, EDGE, q)

        @pl.when(q + 2 < NQ)
        def _():
            halo_start(0, x_ref, 0, q + 2)

        inner(p1, p2, q)

        @pl.when(q + 1 < NQ)
        def _():
            inner(p0, p1, q + 1)

    def step_two(q):
        halo_recv(1, p1, EDGE, q)
        outer(p1, p2, q, 2.0 * SIGMA_TWO / HALF_WIDTH, 2)
        halo_start(2, p2, EDGE, q)
        for k in range(1, 4):
            gather(p2, fa, fs, fr, q, k).start()
        keep(p2, fa, fs.at[q, 0], q).start()
        store(q).start()
        inner(p2, im, q)

    def step_three(q):
        halo_recv(2, p2, EDGE, q)
        outer(p2, im, q, 1.0, 0)
        for k in range(1, 4):
            gather(im, ia, gs, gr, q, k).start()
        keep(im, ia, gs.at[q, 0], q).start()

    def pass_on(q):
        keep(p2, fa, fs.at[q, 0], q).wait()
        for k in range(4):
            if k:
                gather(p2, fa, fs, fr, q, k).wait_recv()
            by_row(lambda: cross_high(q, k).start(), lambda: cross_low(q, k).start())

    def image_in(q):
        keep(im, ia, gs.at[q, 0], q).wait()
        for k in range(4):
            if k:
                gather(im, ia, gs, gr, q, k).wait_recv()
            by_row(lambda: cross_image(q, k).start(), None)

    load.wait()
    inner(p0, p1, 0)

    def wave(i):
        for lag, step in enumerate((step_one, step_two, step_three, pass_on, image_in)):
            pl.when((i >= lag) & (i < NQ + lag))(functools.partial(step, i - lag))

    loop(NQ + 4, wave)

    def arrived(q):
        for k in range(4):
            by_row(lambda: cross_low(q, k).wait_recv(), lambda: cross_high(q, k).wait_recv())

    def split(src, height, dst, start, rows):
        flat = src.reshape(W * height, NZ)

        def body(c):
            v = [flat[pl.ds(start + 2 * c + i, W, stride=height), :] for i in range(2)]
            v = jnp.concatenate(v, 1)
            hi = v.astype(BF16)
            at = pl.ds(pl.multiple_of(c * 2 * NZ, 2 * NZ), 2 * NZ)
            dst[0:W, at] = hi
            dst[128 : 128 + W, at] = (v - hi.astype(F32)).astype(BF16)

        loop(rows // 2, body)

    def mul(a, b):
        g = lax.dot_general(a, b, (((1,), (1,)), ((), ())), preferred_element_type=F32)
        g = g[:128] + g[128:]
        return g[:, :128] + g[:, 128:]

    def put(m, h, g):
        snd_own[:, 2 * m + h] = g[:W].reshape(NX4, ORB, 128)
        if h:
            snd_x[:, m] = jnp.transpose(g)[:W].reshape(NX4, ORB, 128)

    split(fa, XR, fb, 0, XR)
    put(1, 0, mul(fb[...], fb[...]))
    split(ia, XR, ib, 0, XR)
    put(0, 0, mul(ib[...], fb[...]))
    loop(NQ, arrived)

    def across_zero():
        split(fo, XA, ob, 0, XA)
        put(1, 1, mul(fb[:, : XA * NZ], ob[...]))

    def across_one():
        split(fo, XA, ob, 0, XB)
        put(1, 1, mul(fb[:, XA * NZ :], ob[:, : XB * NZ]))

    by_row(across_zero, across_one)

    def image_zero():
        put(0, 1, mul(ib[:, : XA * NZ], ob[...]))

    def image_one():
        def wait(q):
            for k in range(4):
                cross_image(q, k).wait_recv()

        loop(NQ, wait)
        split(fo, XA, ob, XB, XB)
        put(0, 1, mul(fb[:, XA * NZ :], ob[:, : XB * NZ]))

    by_row(image_zero, image_one)

    def rows_own(k):
        return remote(
            snd_own.at[xpeer(k)], rcv_own.at[k], r1s.at[k], r1r.at[k], (dom, row * NX4 + xpeer(k))
        )

    def rows_x(k):
        return remote(
            snd_x.at[xpeer(k)], rcv_x.at[k], r1s.at[4 + k], r1r.at[4 + k], (dom, other + xpeer(k))
        )

    for k in range(4):
        rows_x(k).start()
    for k in range(1, 4):
        rows_own(k).start()
    total = snd_own[xx]
    for k in range(1, 4):
        rows_own(k).wait_recv()
        total = total + rcv_own[k]
    cr = jnp.zeros((2, ORB, 128), F32)
    for k in range(4):
        rows_x(k).wait_recv()
        cr = cr + rcv_x[k]
    red[...] = total
    red[1] = total[1] + cr[0]
    red[3] = total[3] + cr[1]

    def quarter(k):
        t = lax.rem(tt + k, 4)
        return remote(red.at[t], a2.at[k], r2s.at[k], r2r.at[k], (zz * 4 + t, orb))

    for k in range(1, 4):
        quarter(k).start()
    s = red[tt]
    for k in range(1, 4):
        quarter(k).wait_recv()
        s = s + a2[k]
    mine[...] = s

    def along(k):
        z = lax.rem(zz + k, 8)
        return remote(mine, a3.at[k], r3s.at[k], r3r.at[k], (z * 4 + tt, orb))

    for k in range(1, 8):
        along(k).start()
    for k in range(1, 8):
        along(k).wait_recv()
        s = s + a3[k]
    gram_ref[tt] = s

    def back(k):
        t = lax.rem(tt + k, 4)
        return remote(gram_ref.at[tt], gram_ref.at[tt], r4s.at[k], r4r.at[k], (zz * 4 + t, orb))

    for k in range(1, 4):
        back(k).start()

    def sent(q):
        halo_sent(0, x_ref, 0, q)
        halo_sent(1, p1, EDGE, q)
        halo_sent(2, p2, EDGE, q)
        store(q).wait()
        for k in range(1, 4):
            gather(p2, fa, fs, fr, q, k).wait_send()
            gather(im, ia, gs, gr, q, k).wait_send()
        for k in range(4):
            by_row(lambda: cross_high(q, k).wait_send(), lambda: cross_low(q, k).wait_send())
            by_row(lambda: cross_image(q, k).wait_send(), None)

    loop(NQ, sent)
    for k in range(1, 4):
        rows_own(k).wait_send()
        quarter(k).wait_send()
        back(k).wait_send()
    for k in range(4):
        rows_x(k).wait_send()
    for k in range(1, 8):
        along(k).wait_send()
    for k in range(1, 4):
        t = lax.rem(tt + 4 - k, 4)
        remote(
            gram_ref.at[t], gram_ref.at[t], r4s.at[k], r4r.at[k], (zz * 4 + t, orb)
        ).wait_recv()


def finish(full_ref, gram_ref, out_ref, h_ref, s_ref, hold, gram, pair, sem, small):
    def copies(i):
        part = pl.ds(3 * i, 3)
        return (
            pltpu.make_async_copy(full_ref.at[part], hold.at[part], sem.at[0, i]),
            pltpu.make_async_copy(hold.at[part], out_ref.at[part], sem.at[1, i]),
        )

    load = pltpu.make_async_copy(gram_ref, gram, small.at[0])
    load.start()
    for i in range(8):
        copies(i)[0].start()
    for i in range(4):
        copies(i)[0].wait()
        copies(i)[1].start()
    load.wait()
    first = lax.axis_index("orb") < NX4
    scale = 1.0 / (ROWS * NZ * NDOM)
    stores = []
    for m, ref in enumerate((h_ref, s_ref)):
        own, across = gram[2 * m] * scale, gram[2 * m + 1] * scale
        low = jnp.where(first, own, across)
        high = jnp.where(first, across, own)
        pair[m] = jnp.concatenate([low[:, :W], high[:, :W]], 1)
        stores.append(pltpu.make_async_copy(pair.at[m], ref, small.at[1 + m]))
        stores[m].start()
    for i in range(4, 8):
        copies(i)[0].wait()
        copies(i)[1].start()
    for i in range(8):
        copies(i)[1].wait()
    for c in stores:
        c.wait()


def on_device(orbitals, potential, proj_index, proj_values, proj_energy):
    wz, cy = constants()
    dma = pltpu.SemaphoreType.DMA
    vmem = pl.BlockSpec(memory_space=pltpu.VMEM)
    smem = pl.BlockSpec(memory_space=pltpu.SMEM)
    hbm = pl.BlockSpec(memory_space=pl.ANY)
    filtered, gram = pl.pallas_call(
        kernel,
        out_shape=(
            jax.ShapeDtypeStruct((ORB, ROWS, NZ), F32),
            jax.ShapeDtypeStruct((4, ORB, 128), F32),
        ),
        in_specs=[hbm, vmem, smem, smem, smem, vmem, vmem],
        out_specs=(hbm, vmem),
        scratch_shapes=[
            pltpu.VMEM((ORB, PAD, NZ), F32),
            pltpu.VMEM((ORB, PAD, NZ), F32),
            pltpu.VMEM((ORB, PAD, NZ), F32),
            pltpu.VMEM((ORB, PAD, NZ), F32),
            pltpu.VMEM((ROWS, NZ), F32),
            pltpu.VMEM((4, 6, NY, NZ), F32),
            pltpu.VMEM((2, 29, NY, NZ), F32),
            pltpu.VMEM((2, 10, NY, NZ), F32),
            pltpu.VMEM((ORB, 4, NY, NZ), F32),
            pltpu.VMEM((ORB, 4, NY, NZ), F32),
            pltpu.VMEM((W, XR, NZ), F32),
            pltpu.VMEM((W, XR, NZ), F32),
            pltpu.VMEM((W, XA, NZ), F32),
            pltpu.VMEM((256, K), BF16),
            pltpu.VMEM((256, K), BF16),
            pltpu.VMEM((256, XA * NZ), BF16),
            pltpu.VMEM((NX4, 4, ORB, 128), F32),
            pltpu.VMEM((NX4, 2, ORB, 128), F32),
            pltpu.VMEM((NX4, 4, ORB, 128), F32),
            pltpu.VMEM((NX4, 2, ORB, 128), F32),
            pltpu.VMEM((4, ORB, 128), F32),
            pltpu.VMEM((4, ORB, 128), F32),
            pltpu.VMEM((8, ORB, 128), F32),
            pltpu.VMEM((ORB, 128), F32),
            dma((1 + NQ,)),
            dma((3, 2, NQ)), dma((3, 2, NQ)),
            dma((NQ, 4)), dma((NQ, 4)),
            dma((NQ, 4)), dma((NQ, 4)),
            dma((NQ, 4)), dma((NQ, 4)),
            dma((NQ, 4)), dma((NQ, 4)),
            dma((8,)), dma((8,)),
            dma((4,)), dma((4,)),
            dma((8,)), dma((8,)),
            dma((4,)), dma((4,)),
        ],
        compiler_params=pltpu.CompilerParams(
            collective_id=0, has_side_effects=True, vmem_limit_bytes=56 << 20
        ),
        name="filter_step",
    )(
        orbitals.reshape(ORB, ROWS, NZ),
        potential.reshape(ROWS, NZ),
        proj_index,
        proj_values,
        proj_energy.reshape(1, -1),
        wz,
        cy,
    )
    filtered, ham, corr = pl.pallas_call(
        finish,
        out_shape=(
            jax.ShapeDtypeStruct((ORB, ROWS, NZ), F32),
            jax.ShapeDtypeStruct((ORB, 2 * W), F32),
            jax.ShapeDtypeStruct((ORB, 2 * W), F32),
        ),
        in_specs=[hbm, hbm],
        out_specs=(hbm, hbm, hbm),
        scratch_shapes=[
            pltpu.VMEM((ORB, ROWS, NZ), F32),
            pltpu.VMEM((4, ORB, 128), F32),
            pltpu.VMEM((2, ORB, 2 * W), F32),
            dma((2, 8)),
            dma((3,)),
        ],
        name="outputs",
    )(filtered, gram)
    return filtered.reshape(orbitals.shape), ham, corr


def solution(mesh):
    in_specs = (P("orb", "dom", None, None), P("dom", None, None), P(), P(), P())
    out_specs = (P("orb", "dom", None, None), P("orb", None), P("orb", None))
    return jax.shard_map(
        on_device, mesh=mesh, in_specs=in_specs, out_specs=out_specs, check_vma=False
    )
```

```python
import functools

import jax
import jax.numpy as jnp
import numpy as np
from jax import lax
from jax.experimental import pallas as pl
from jax.experimental.pallas import tpu as pltpu
from jax.sharding import PartitionSpec as P

MESH = pl.DeviceIdType.MESH
F32 = jnp.float32
BF16 = jnp.bfloat16

CENTER_WEIGHT = -5369.0 / 1800.0
SIDE_WEIGHTS = (12.0 / 7.0, -15.0 / 56.0, 10.0 / 189.0, -1.0 / 112.0, 2.0 / 1925.0, -1.0 / 16632.0)
LOWER_BOUND = -1.0
CUT_BOUND = 2.0
UPPER_BOUND = 16.0
HALF_WIDTH = (UPPER_BOUND - CUT_BOUND) / 2.0
MIDDLE = (UPPER_BOUND + CUT_BOUND) / 2.0
SIGMA_ONE = HALF_WIDTH / (LOWER_BOUND - MIDDLE)
SIGMA_TWO = 1.0 / (2.0 / SIGMA_ONE - SIGMA_ONE)

ORB = 24
CX = 24
HALO = 6
NY = 8
NZ = 128
ROWS = CX * NY
EDGE = HALO * NY
PAD = ROWS + 2 * EDGE
NQ = 4
OQ = ORB // NQ
NX4 = 4
XL = CX // NX4
XR = XL * NY
XA, XB = 32, 16
W = NX4 * ORB
K = XR * NZ
NDOM = 32
SIDE = tuple(-0.5 * w for w in SIDE_WEIGHTS)
DIAG = -0.5 * 3.0 * CENTER_WEIGHT


def band(n):
    m = np.zeros((n, n), np.float64)
    for k, w in enumerate(SIDE, 1):
        m += w * (np.eye(n, k=k) + np.eye(n, k=-k))
    return m


def constants():
    bz = jnp.asarray(band(NZ), F32)
    hi = bz.astype(BF16)
    lo = (bz - hi.astype(F32)).astype(BF16)
    wz = jnp.concatenate(
        [jnp.concatenate([hi, lo], 1), jnp.concatenate([hi, jnp.zeros_like(lo)], 1)], 0
    )
    by = band(NY)
    cy = np.zeros((NY, NY, NZ), np.float32)
    for s in range(NY):
        for y in range(NY):
            cy[s, y, :] = by[y, (y - s) % NY]
    return wz, jnp.asarray(cy)


def kernel(
    x_ref, pot_ref, idx_ref, val_ref, en_ref, wz_ref, cy_ref,
    out_ref, gram_ref,
    p0, p1, p2, im, cf, box, dfo, dfp, tb, pe,
    fa, ia, fo, fb, ib, ob, snd_own, snd_x, rcv_own, rcv_x, red, a2, a3, mine,
    loc_sem, hs, hr, fs, fr, gs, gr, ys, yr, vs, vr, r1s, r1r, r2s, r2r, r3s, r3r, r4s, r4r,
):
    dom = lax.axis_index("dom")
    orb = lax.axis_index("orb")
    row = orb // NX4
    xx = orb % NX4
    zz = dom // 4
    tt = dom % 4
    up = lax.rem(dom + 1, NDOM)
    down = lax.rem(dom + NDOM - 1, NDOM)
    other = (1 - row) * NX4

    def xpeer(k):
        return lax.rem(xx + k, NX4)

    barrier = pltpu.get_barrier_semaphore()
    peers = [(up, orb), (down, orb)]
    peers += [(dom, row * NX4 + xpeer(k)) for k in range(1, 4)]
    peers += [(dom, other + xpeer(k)) for k in range(4)]
    peers += [(zz * 4 + lax.rem(tt + k, 4), orb) for k in range(1, 4)]
    peers += [(lax.rem(zz + k, 8) * 4 + tt, orb) for k in range(1, 8)]
    for peer in peers:
        pl.semaphore_signal(barrier, inc=1, device_id=peer, device_id_type=MESH)

    load = pltpu.make_async_copy(x_ref, p0.at[:, pl.ds(EDGE, ROWS), :], loc_sem.at[0])
    load.start()
    pl.semaphore_wait(barrier, len(peers))

    def remote(src, dst, send, recv, device):
        return pltpu.make_async_remote_copy(
            src_ref=src, dst_ref=dst, send_sem=send, recv_sem=recv, device_id=device, device_id_type=MESH
        )

    def halo(field, src, base, q, way):
        part = pl.ds(q * OQ, OQ)
        if way == 0:
            s = src.at[part, pl.ds(base + ROWS - EDGE, EDGE), :]
            d = (p0, p1, p2)[field].at[part, pl.ds(0, EDGE), :]
            to = (up, orb)
        else:
            s = src.at[part, pl.ds(base, EDGE), :]
            d = (p0, p1, p2)[field].at[part, pl.ds(EDGE + ROWS, EDGE), :]
            to = (down, orb)
        return remote(s, d, hs.at[field, way, q], hr.at[field, way, q], to)

    def halo_start(field, src, base, q):
        @pl.when(dom < NDOM - 1)
        def _():
            halo(field, src, base, q, 0).start()

        @pl.when(dom > 0)
        def _():
            halo(field, src, base, q, 1).start()

    def halo_recv(field, src, base, q):
        @pl.when(dom > 0)
        def _():
            halo(field, src, base, q, 0).wait_recv()

        @pl.when(dom < NDOM - 1)
        def _():
            halo(field, src, base, q, 1).wait_recv()

    def halo_sent(field, src, base, q):
        @pl.when(dom < NDOM - 1)
        def _():
            halo(field, src, base, q, 0).wait_send()

        @pl.when(dom > 0)
        def _():
            halo(field, src, base, q, 1).wait_send()

    def loop(n, body):
        lax.fori_loop(0, n, lambda i, c: (body(i), c)[1], 0)

    loop(2, lambda q: halo_start(0, x_ref, 0, q))

    @pl.when(dom == 0)
    def _():
        for p in (p0, p1, p2):
            p[:, 0:EDGE, :] = jnp.zeros((ORB, EDGE, NZ), F32)

    @pl.when(dom == NDOM - 1)
    def _():
        for p in (p0, p1, p2):
            p[:, EDGE + ROWS :, :] = jnp.zeros((ORB, EDGE, NZ), F32)

    cf[...] = pot_ref[...] + (DIAG - MIDDLE)
    for buf in (fb, ib, ob):
        for h in (0, 128):
            buf[h + W : h + 128, :] = jnp.zeros((128 - W, buf.shape[1]), BF16)

    sub = lax.broadcasted_iota(jnp.int32, (NY, NZ), 0)
    lane = lax.broadcasted_iota(jnp.int32, (NY, NZ), 1)

    def atom_id(a):
        return jnp.where(a < 2, 2 * dom + a, jnp.maximum(2 * dom - 4 + a, 0))

    def start_of(a):
        first = idx_ref[atom_id(a), 0]
        return first // (NY * NZ) - CX * dom, first // NZ % NY, first % NZ

    def build_box(a):
        _, y0, z0 = start_of(a)
        dy = sub - y0
        dz = lane - z0

        def layer(l):
            d = jnp.zeros((NY, NZ), F32)
            for j in range(4):
                for k in range(4):
                    d = jnp.where((dy == j) & (dz == k), val_ref[atom_id(a), l * 16 + j * 4 + k], d)
            box[a, l] = d

        loop(6, layer)

    loop(4, build_box)

    def place(a, x):
        x0, _, _ = start_of(a)
        off = jnp.zeros((NY, NZ), jnp.int32) + (x - x0)
        d = jnp.zeros((NY, NZ), F32)
        for l in range(6):
            d = jnp.where(off == l, box[a, l], d)
        return d

    def place_own(x):
        for a in range(2):
            dfo[a, x] = place(a, x)

    def place_low(i):
        for a in range(2):
            dfp[a, i] = place(a + 2, i - 5)

    loop(29, place_own)
    loop(10, place_low)

    def inner(p, n, q):
        def body(i):
            o = q * OQ + i
            c = p[o, EDGE : EDGE + ROWS, :]
            hi = c.astype(BF16)
            lo = (c - hi.astype(F32)).astype(BF16)
            z = jnp.dot(jnp.concatenate([hi, lo], 1), wz_ref[...], preferred_element_type=F32)
            z = z[:, :NZ] + z[:, NZ:]
            t = [jnp.zeros((NY, NZ), F32)] * 4
            for x0 in range(0, CX, 8):
                first, last = max(x0 - HALO, 0), min(x0 + 8 + HALO, CX)
                blk = p[o, EDGE + first * NY : EDGE + last * NY, :].reshape(last - first, NY, NZ)
                zero = jnp.zeros((8 + 2 * HALO - (last - first), NY, NZ), F32)
                if x0 - HALO < 0:
                    blk = jnp.concatenate([zero, blk], 0)
                elif x0 + 8 + HALO > CX:
                    blk = jnp.concatenate([blk, zero], 0)
                ctr = blk[HALO : HALO + 8]
                rows = slice(x0 * NY, (x0 + 8) * NY)
                s = cf[rows, :].reshape(8, NY, NZ) * ctr + z[rows, :].reshape(8, NY, NZ)
                for k in range(1, HALO + 1):
                    s = s + SIDE[k - 1] * (blk[HALO + k : HALO + 8 + k] + blk[HALO - k : HALO + 8 - k])
                for r in range(1, NY):
                    s = s + cy_ref[r][None] * pltpu.roll(ctr, r, 1)
                n[o, pl.ds(EDGE + x0 * NY, 8 * NY), :] = s.reshape(8 * NY, NZ)
                for a in range(2):
                    t[a] = t[a] + jnp.sum(dfo[a, x0 : x0 + 8] * ctr, axis=0)
                    if x0 == 0:
                        t[2 + a] = jnp.sum(dfp[a, 5:10] * ctr[0:5], axis=0)
            for a in range(4):
                tb[o, a] = t[a]

        loop(OQ, body)

    def outer(p, n, q, scale, extra):
        def body(i):
            o = q * OQ + i
            low = p[o, 0:EDGE, :].reshape(HALO, NY, NZ)
            high = p[o, EDGE + ROWS : PAD, :].reshape(HALO, NY, NZ)
            for a in range(2):
                tb[o, a] = tb[o, a] + jnp.sum(dfo[a, 24:29] * high[0:5], axis=0)
                tb[o, 2 + a] = tb[o, 2 + a] + jnp.sum(dfp[a, 0:5] * low[1:6], axis=0)
            first = [jnp.zeros((NY, NZ), F32)] * HALO
            last = [jnp.zeros((NY, NZ), F32)] * HALO
            for k in range(1, HALO + 1):
                for x in range(k):
                    first[x] = first[x] + SIDE[k - 1] * low[HALO - k + x]
                    last[HALO - k + x] = last[HALO - k + x] + SIDE[k - 1] * high[x]
            add = jnp.concatenate(first, 0)
            n[o, pl.ds(EDGE, EDGE), :] = n[o, pl.ds(EDGE, EDGE), :] + add
            add = jnp.concatenate(last, 0)
            n[o, pl.ds(ROWS, EDGE), :] = n[o, pl.ds(ROWS, EDGE), :] + add

        loop(OQ, body)
        part = pl.ds(q * OQ, OQ)
        total = jnp.sum(jnp.sum(tb[part], axis=3, keepdims=True), axis=2, keepdims=True)
        for a in range(4):
            e = en_ref[0, atom_id(a)]
            if a >= 2:
                e = jnp.where(dom > 0, e, 0.0)
            pe[part, a] = jnp.broadcast_to(total[:, a] * e, (OQ, NY, NZ))

        def finish(i):
            o = q * OQ + i
            for x0 in range(0, CX, 8):
                rows = pl.ds(EDGE + x0 * NY, 8 * NY)
                s = n[o, rows, :].reshape(8, NY, NZ)
                for a in range(2):
                    s = s + dfo[a, x0 : x0 + 8] * pe[o, a][None]
                if x0 == 0:
                    t = s[0:5]
                    for a in range(2):
                        t = t + dfp[a, 5:10] * pe[o, 2 + a][None]
                    s = jnp.concatenate([t, s[5:8]], 0)
                if extra == 2:
                    s = scale * s - (SIGMA_ONE * SIGMA_TWO) * p0[o, rows, :].reshape(8, NY, NZ)
                elif extra == 1:
                    s = scale * s
                else:
                    s = s + MIDDLE * p[o, rows, :].reshape(8, NY, NZ)
                n[o, rows, :] = s.reshape(8 * NY, NZ)

        loop(OQ, finish)

    def gather(src, dst, send, recv, q, k):
        s = src.at[pl.ds(q * OQ, OQ), pl.ds(pl.multiple_of(EDGE + xpeer(k) * XR, 8), XR), :]
        d = dst.at[pl.ds(xx * ORB + q * OQ, OQ), :, :]
        return remote(s, d, send.at[q, k], recv.at[q, k], (dom, row * NX4 + xpeer(k)))

    def keep(src, dst, sem, q):
        s = src.at[pl.ds(q * OQ, OQ), pl.ds(pl.multiple_of(EDGE + xx * XR, 8), XR), :]
        return pltpu.make_async_copy(s, dst.at[pl.ds(xx * ORB + q * OQ, OQ), :, :], sem)

    def store(q):
        part = pl.ds(q * OQ, OQ)
        return pltpu.make_async_copy(
            p2.at[part, pl.ds(EDGE, ROWS), :], out_ref.at[part, :, :], loc_sem.at[1 + q]
        )

    def cross(src, to, rows, q, k, send, recv):
        who = lax.rem(xx + NX4 - k, NX4)
        part = pl.ds(who * ORB + q * OQ, OQ)
        return remote(
            src.at[part, rows, :], fo.at[part, to, :], send.at[q, k], recv.at[q, k], (dom, other + xx)
        )

    def cross_low(q, k):
        return cross(fa, pl.ds(0, XA), pl.ds(0, XA), q, k, ys, yr)

    def cross_high(q, k):
        return cross(fa, pl.ds(0, XB), pl.ds(XA, XB), q, k, ys, yr)

    def cross_image(q, k):
        return cross(ia, pl.ds(XB, XB), pl.ds(XA, XB), q, k, vs, vr)

    def by_row(zero, one):
        if zero is not None:
            pl.when(row == 0)(zero)
        if one is not None:
            pl.when(row == 1)(one)

    def step_one(q):
        halo_recv(0, x_ref, 0, q)
        outer(p0, p1, q, SIGMA_ONE / HALF_WIDTH, 1)
        halo_start(1, p1, EDGE, q)

        @pl.when(q + 2 < NQ)
        def _():
            halo_start(0, x_ref, 0, q + 2)

        inner(p1, p2, q)

        @pl.when(q + 1 < NQ)
        def _():
            inner(p0, p1, q + 1)

    def step_two(q):
        halo_recv(1, p1, EDGE, q)
        outer(p1, p2, q, 2.0 * SIGMA_TWO / HALF_WIDTH, 2)
        halo_start(2, p2, EDGE, q)
        for k in range(1, 4):
            gather(p2, fa, fs, fr, q, k).start()
        keep(p2, fa, fs.at[q, 0], q).start()
        store(q).start()
        inner(p2, im, q)

    def step_three(q):
        halo_recv(2, p2, EDGE, q)
        outer(p2, im, q, 1.0, 0)
        for k in range(1, 4):
            gather(im, ia, gs, gr, q, k).start()
        keep(im, ia, gs.at[q, 0], q).start()

    def pass_on(q):
        keep(p2, fa, fs.at[q, 0], q).wait()
        for k in range(4):
            if k:
                gather(p2, fa, fs, fr, q, k).wait_recv()
            by_row(lambda: cross_high(q, k).start(), lambda: cross_low(q, k).start())

    def image_in(q):
        keep(im, ia, gs.at[q, 0], q).wait()
        for k in range(4):
            if k:
                gather(im, ia, gs, gr, q, k).wait_recv()
            by_row(lambda: cross_image(q, k).start(), None)

    load.wait()
    inner(p0, p1, 0)

    def wave(i):
        for lag, step in enumerate((step_one, step_two, step_three, pass_on, image_in)):
            pl.when((i >= lag) & (i < NQ + lag))(functools.partial(step, i - lag))

    loop(NQ + 4, wave)

    def arrived(q):
        for k in range(4):
            by_row(lambda: cross_low(q, k).wait_recv(), lambda: cross_high(q, k).wait_recv())

    def split(src, height, dst, start, rows):
        flat = src.reshape(W * height, NZ)

        def body(c):
            v = [flat[pl.ds(start + 2 * c + i, W, stride=height), :] for i in range(2)]
            v = jnp.concatenate(v, 1)
            hi = v.astype(BF16)
            at = pl.ds(pl.multiple_of(c * 2 * NZ, 2 * NZ), 2 * NZ)
            dst[0:W, at] = hi
            dst[128 : 128 + W, at] = (v - hi.astype(F32)).astype(BF16)

        loop(rows // 2, body)

    def mul(a, b):
        g = lax.dot_general(a, b, (((1,), (1,)), ((), ())), preferred_element_type=F32)
        g = g[:128] + g[128:]
        return g[:, :128] + g[:, 128:]

    def put(m, h, g):
        snd_own[m, :, h] = g[:W].reshape(NX4, ORB, 128)
        if h:
            snd_x[m] = jnp.transpose(g)[:W].reshape(NX4, ORB, 128)

    def rows_own(m, k):
        to = (dom, row * NX4 + xpeer(k))
        return remote(snd_own.at[m, xpeer(k)], rcv_own.at[m, k], r1s.at[m, k], r1r.at[m, k], to)

    def rows_x(m, k):
        to = (dom, other + xpeer(k))
        return remote(snd_x.at[m, xpeer(k)], rcv_x.at[m, k], r1s.at[m, 4 + k], r1r.at[m, 4 + k], to)

    def send_rows(m):
        for k in range(4):
            rows_x(m, k).start()
        for k in range(1, 4):
            rows_own(m, k).start()

    def add_rows(m):
        own = snd_own[m, xx]
        for k in range(1, 4):
            rows_own(m, k).wait_recv()
            own = own + rcv_own[m, k]
        cr = own[1]
        for k in range(4):
            rows_x(m, k).wait_recv()
            cr = cr + rcv_x[m, k]
        red[2 * m] = own[0]
        red[2 * m + 1] = cr

    split(fa, XR, fb, 0, XR)
    put(1, 0, mul(fb[...], fb[...]))
    split(ia, XR, ib, 0, XR)
    put(0, 0, mul(ib[...], fb[...]))
    loop(NQ, arrived)

    def across_zero():
        split(fo, XA, ob, 0, XA)
        put(1, 1, mul(fb[:, : XA * NZ], ob[...]))

    def across_one():
        split(fo, XA, ob, 0, XB)
        put(1, 1, mul(fb[:, XA * NZ :], ob[:, : XB * NZ]))

    by_row(across_zero, across_one)
    send_rows(1)

    def image_zero():
        put(0, 1, mul(ib[:, : XA * NZ], ob[...]))

    def image_one():
        def wait(q):
            for k in range(4):
                cross_image(q, k).wait_recv()

        loop(NQ, wait)
        split(fo, XA, ob, XB, XB)
        put(0, 1, mul(fb[:, XA * NZ :], ob[:, : XB * NZ]))

    by_row(image_zero, image_one)
    send_rows(0)
    add_rows(1)
    add_rows(0)

    def quarter(k):
        t = lax.rem(tt + k, 4)
        return remote(red.at[t], a2.at[k], r2s.at[k], r2r.at[k], (zz * 4 + t, orb))

    for k in range(1, 4):
        quarter(k).start()
    s = red[tt]
    for k in range(1, 4):
        quarter(k).wait_recv()
        s = s + a2[k]
    mine[...] = s

    def along(k):
        z = lax.rem(zz + k, 8)
        return remote(mine, a3.at[k], r3s.at[k], r3r.at[k], (z * 4 + tt, orb))

    for k in range(1, 8):
        along(k).start()
    for k in range(1, 8):
        along(k).wait_recv()
        s = s + a3[k]
    gram_ref[tt] = s

    def back(k):
        t = lax.rem(tt + k, 4)
        return remote(gram_ref.at[tt], gram_ref.at[tt], r4s.at[k], r4r.at[k], (zz * 4 + t, orb))

    for k in range(1, 4):
        back(k).start()

    def sent(q):
        halo_sent(0, x_ref, 0, q)
        halo_sent(1, p1, EDGE, q)
        halo_sent(2, p2, EDGE, q)
        store(q).wait()
        for k in range(1, 4):
            gather(p2, fa, fs, fr, q, k).wait_send()
            gather(im, ia, gs, gr, q, k).wait_send()
        for k in range(4):
            by_row(lambda: cross_high(q, k).wait_send(), lambda: cross_low(q, k).wait_send())
            by_row(lambda: cross_image(q, k).wait_send(), None)

    loop(NQ, sent)
    for m in range(2):
        for k in range(1, 4):
            rows_own(m, k).wait_send()
        for k in range(4):
            rows_x(m, k).wait_send()
    for k in range(1, 4):
        quarter(k).wait_send()
        back(k).wait_send()
    for k in range(1, 8):
        along(k).wait_send()
    for k in range(1, 4):
        t = lax.rem(tt + 4 - k, 4)
        remote(
            gram_ref.at[t], gram_ref.at[t], r4s.at[k], r4r.at[k], (zz * 4 + t, orb)
        ).wait_recv()


def finish(full_ref, gram_ref, out_ref, h_ref, s_ref, hold, gram, pair, sem, small):
    def copies(i):
        part = pl.ds(3 * i, 3)
        return (
            pltpu.make_async_copy(full_ref.at[part], hold.at[part], sem.at[0, i]),
            pltpu.make_async_copy(hold.at[part], out_ref.at[part], sem.at[1, i]),
        )

    load = pltpu.make_async_copy(gram_ref, gram, small.at[0])
    load.start()
    for i in range(8):
        copies(i)[0].start()
    for i in range(4):
        copies(i)[0].wait()
        copies(i)[1].start()
    load.wait()
    first = lax.axis_index("orb") < NX4
    scale = 1.0 / (ROWS * NZ * NDOM)
    stores = []
    for m, ref in enumerate((h_ref, s_ref)):
        own, across = gram[2 * m] * scale, gram[2 * m + 1] * scale
        low = jnp.where(first, own, across)
        high = jnp.where(first, across, own)
        pair[m] = jnp.concatenate([low[:, :W], high[:, :W]], 1)
        stores.append(pltpu.make_async_copy(pair.at[m], ref, small.at[1 + m]))
        stores[m].start()
    for i in range(4, 8):
        copies(i)[0].wait()
        copies(i)[1].start()
    for i in range(8):
        copies(i)[1].wait()
    for c in stores:
        c.wait()


def on_device(orbitals, potential, proj_index, proj_values, proj_energy):
    wz, cy = constants()
    dma = pltpu.SemaphoreType.DMA
    vmem = pl.BlockSpec(memory_space=pltpu.VMEM)
    smem = pl.BlockSpec(memory_space=pltpu.SMEM)
    hbm = pl.BlockSpec(memory_space=pl.ANY)
    filtered, gram = pl.pallas_call(
        kernel,
        out_shape=(
            jax.ShapeDtypeStruct((ORB, ROWS, NZ), F32),
            jax.ShapeDtypeStruct((4, ORB, 128), F32),
        ),
        in_specs=[hbm, vmem, smem, smem, smem, vmem, vmem],
        out_specs=(hbm, vmem),
        scratch_shapes=[
            pltpu.VMEM((ORB, PAD, NZ), F32),
            pltpu.VMEM((ORB, PAD, NZ), F32),
            pltpu.VMEM((ORB, PAD, NZ), F32),
            pltpu.VMEM((ORB, PAD, NZ), F32),
            pltpu.VMEM((ROWS, NZ), F32),
            pltpu.VMEM((4, 6, NY, NZ), F32),
            pltpu.VMEM((2, 29, NY, NZ), F32),
            pltpu.VMEM((2, 10, NY, NZ), F32),
            pltpu.VMEM((ORB, 4, NY, NZ), F32),
            pltpu.VMEM((ORB, 4, NY, NZ), F32),
            pltpu.VMEM((W, XR, NZ), F32),
            pltpu.VMEM((W, XR, NZ), F32),
            pltpu.VMEM((W, XA, NZ), F32),
            pltpu.VMEM((256, K), BF16),
            pltpu.VMEM((256, K), BF16),
            pltpu.VMEM((256, XA * NZ), BF16),
            pltpu.VMEM((2, NX4, 2, ORB, 128), F32),
            pltpu.VMEM((2, NX4, ORB, 128), F32),
            pltpu.VMEM((2, NX4, 2, ORB, 128), F32),
            pltpu.VMEM((2, NX4, ORB, 128), F32),
            pltpu.VMEM((4, ORB, 128), F32),
            pltpu.VMEM((4, ORB, 128), F32),
            pltpu.VMEM((8, ORB, 128), F32),
            pltpu.VMEM((ORB, 128), F32),
            dma((1 + NQ,)),
            dma((3, 2, NQ)), dma((3, 2, NQ)),
            dma((NQ, 4)), dma((NQ, 4)),
            dma((NQ, 4)), dma((NQ, 4)),
            dma((NQ, 4)), dma((NQ, 4)),
            dma((NQ, 4)), dma((NQ, 4)),
            dma((2, 8)), dma((2, 8)),
            dma((4,)), dma((4,)),
            dma((8,)), dma((8,)),
            dma((4,)), dma((4,)),
        ],
        compiler_params=pltpu.CompilerParams(
            collective_id=0, has_side_effects=True, vmem_limit_bytes=56 << 20
        ),
        name="filter_step",
    )(
        orbitals.reshape(ORB, ROWS, NZ),
        potential.reshape(ROWS, NZ),
        proj_index,
        proj_values,
        proj_energy.reshape(1, -1),
        wz,
        cy,
    )
    filtered, ham, corr = pl.pallas_call(
        finish,
        out_shape=(
            jax.ShapeDtypeStruct((ORB, ROWS, NZ), F32),
            jax.ShapeDtypeStruct((ORB, 2 * W), F32),
            jax.ShapeDtypeStruct((ORB, 2 * W), F32),
        ),
        in_specs=[hbm, hbm],
        out_specs=(hbm, hbm, hbm),
        scratch_shapes=[
            pltpu.VMEM((ORB, ROWS, NZ), F32),
            pltpu.VMEM((4, ORB, 128), F32),
            pltpu.VMEM((2, ORB, 2 * W), F32),
            dma((2, 8)),
            dma((3,)),
        ],
        name="outputs",
    )(filtered, gram)
    return filtered.reshape(orbitals.shape), ham, corr


def solution(mesh):
    in_specs = (P("orb", "dom", None, None), P("dom", None, None), P(), P(), P())
    out_specs = (P("orb", "dom", None, None), P("orb", None), P("orb", None))
    return jax.shard_map(
        on_device, mesh=mesh, in_specs=in_specs, out_specs=out_specs, check_vma=False
    )
```
